1024 devices in a mesh: scen: 128 (over x, y, core), arc: 8 (over z).
Axes of the slice: x: 8, y: 8, z: 8, core: 2. Of those that a mesh axis runs over, the one named last changes fastest.
Arguments:
- coupling: bfloat16 [1024, 4096], P(None, 'arc'), may hold values from -0.09375 to 0.09375
- incidence: int32 [8, 32], P(None, 'arc'), may hold values 0 or 1
- arc_cost: float32 [4096], P('arc'), may hold values from -6 to 6
- capacity: float32 [4096], P('arc'), may hold values from 0.5 to 2
- demand: float32 [128, 1024], P('scen'), may hold values from -4 to 4
- weights: int32 [128], P('scen'), may hold values from 128 to 24448, as said below
- fleet_slots: int32 [1024], P('arc'), may hold values from 0 to 511, as said below
Outputs:
- flows: float32 [128, 4096], P('scen', 'arc')
- duals: float32 [128, 1024], P('scen', 'arc')
- multipliers: float32 [128, 1024], P('scen', 'arc')
- consensus: float32 [1024], P('arc')
- spread: float32 [2], replicated
The draws below stay inside these ranges and needn't reach their ends.
Inputs may be any that keep to these rules, and one draw needn't show every extreme that they name: `weights`: weight s is (128 + 2 s) times a power of two from 1 to 64. `fleet_slots`: within each aligned block of 128 entries (one arc block) the values are distinct positions inside that arc block.
All inputs are finite; a program needn't handle non-finite values. No bound on the sum of `incidence` on one device may be relied on, other than what follows from the above.
Results may differ from the reference program's by a relative error of at most 0.012.
Values may be sent and summed in bfloat16 or wider, within the bound.
A program may use at most 32 MiB of HBM per device.

```python
import jax
import jax.numpy as jnp
from jax import lax

A_DEV = 512
TILE = 128
ITERS = 4
ROUNDS = 2
F_DEV = 128
SCEN = 128
NA = 4096
ROWS = 1024
NF = 1024


def draw_weights(key, part):
    index = jnp.arange(SCEN, dtype=jnp.int32)
    powers = jax.random.randint(key, (SCEN,), 0, 7, dtype=jnp.int32)
    powers = jnp.where(index == 0, 0, jnp.where(index == SCEN - 1, 6, powers)).astype(jnp.int32)
    factor = jnp.left_shift(jnp.ones((SCEN,), jnp.int32), powers)
    return ((SCEN + 2 * index) * factor).astype(jnp.int32)


def draw_fleet_slots(key, part):

    def one_block(block_key):
        first_key, second_key = jax.random.split(block_key)
        inner = jax.random.permutation(first_key, A_DEV - 2)[:F_DEV - 2].astype(jnp.int32) + 1
        values = jnp.concatenate([jnp.array([0, A_DEV - 1], jnp.int32), inner])
        order = jax.random.permutation(second_key, F_DEV).astype(jnp.int32)
        return values[order]
    block_keys = jax.random.split(key, NF // F_DEV)
    return jax.vmap(one_block)(block_keys).reshape(-1).astype(jnp.int32)


def with_ends(drawn, rng, least, largest):
    longest = drawn.shape.index(max(drawn.shape))
    spots = []
    for shift in (0, 1):
        where = [jax.random.randint(jax.random.fold_in(rng, axis), (), 0, length) for axis, length in enumerate(drawn.shape)]
        where[longest] = (where[longest] + shift) % drawn.shape[longest]
        spots.append(tuple(where))
    return drawn.at[spots[0]].set(least).at[spots[1]].set(largest)


def levels(own_key, shape, pieces, least, largest):
    def one(position, shards_of):
        heights = jax.random.uniform(jax.random.fold_in(jax.random.fold_in(own_key, 6), position), (shards_of,), jnp.float32, least / len(pieces), largest / len(pieces))
        return jnp.repeat(jnp.exp(heights), shape[position] // shards_of).reshape((-1,) + (1,) * (len(shape) - position - 1))

    gain = one(*pieces[0])
    for cut in pieces[1:]:
        gain = gain * one(*cut)
    return gain


def noise(own_key, shape, scale, reach, pieces=(), kind=jnp.bfloat16):
    result = jax.random.normal(own_key, shape, jnp.float32) * scale
    if len(pieces) > 0:
        result = levels(own_key, shape, pieces, -0.22, 0.18) * result
    return jnp.clip(result, min=-reach, max=reach).astype(kind)


def setup_inputs(seed: int = 0) -> dict:
    keys = jax.random.split(jax.random.key(seed), 8)
    return {
        "coupling": noise(keys[0], (ROWS, NA), NA ** -0.5, 0.09375, ((1, 8),)),
        "incidence": with_ends((jax.random.randint(keys[1], (ROWS // TILE, NA // TILE), 0, 2) < 1).astype(jnp.int32), jax.random.fold_in(keys[1], 1), 0, 1),
        "arc_cost": noise(keys[2], (NA,), 1.0, 6.0, ((0, 8),), jnp.float32),
        "capacity": jnp.clip(0.5 + 1.5 * jax.random.uniform(keys[3], (NA,), jnp.float32) ** levels(keys[3], (NA,), ((0, 8),), -0.2, 0.2), 0.5, 2.0),
        "demand": noise(keys[4], (SCEN, ROWS), 0.5, 4.0, ((0, 128),), jnp.float32),
        "weights": draw_weights(jax.random.fold_in(keys[7], 71), 0),
        "fleet_slots": draw_fleet_slots(jax.random.fold_in(keys[7], 71), 0),
    }


primal_step = 0.9
dual_step = 0.9
penalty = 1.0

def reference(coupling, incidence, arc_cost, capacity, demand, weights, fleet_slots):
    total_rows, total_arcs = coupling.shape
    masked = (coupling.reshape(total_rows // TILE, TILE, total_arcs // TILE, TILE) * incidence.astype(jnp.bfloat16)[:, None, :, None]).reshape(total_rows, total_arcs)
    block_owner = jnp.arange(NF, dtype=jnp.int32) // F_DEV
    slot_index = (fleet_slots + block_owner * A_DEV).astype(jnp.int32)
    shares = weights.astype(jnp.float32)
    weight_sum = jnp.sum(shares)
    flows = jnp.zeros((SCEN, NA), jnp.float32)
    duals = jnp.zeros((SCEN, ROWS), jnp.float32)
    multipliers = jnp.zeros((SCEN, NF), jnp.float32)
    consensus = jnp.zeros((NF,), jnp.float32)
    spreads = []
    for round_index in range(ROUNDS):
        for step_index in range(ITERS):
            dual_pull = jnp.dot(duals.astype(jnp.bfloat16), masked, preferred_element_type=jnp.float32)
            fleet_push = multipliers + penalty * (flows[:, slot_index] - consensus[None, :])
            gradient = (arc_cost[None, :] + dual_pull).at[:, slot_index].add(fleet_push)
            flows_next = jnp.clip(flows - primal_step * gradient, 0.0, capacity[None, :])
            flows_bar = (2.0 * flows_next - flows).astype(jnp.bfloat16)
            row_load = jnp.dot(flows_bar, masked.T, preferred_element_type=jnp.float32)
            duals = jnp.maximum(duals + dual_step * (row_load - demand), 0.0)
            flows = flows_next
        fleet_flow = flows[:, slot_index]
        consensus = lax.optimization_barrier(jnp.sum(shares[:, None] * fleet_flow, axis=0)) / weight_sum
        deviation = fleet_flow - consensus[None, :]
        spreads.append(jnp.sqrt(jnp.sum(shares[:, None] * deviation * deviation) / (weight_sum * NF) + 1e-06))
        multipliers = multipliers + penalty * deviation
    return (flows, duals, multipliers, consensus, jnp.stack(spreads))
```

```python
import functools

import jax
import jax.numpy as jnp
from jax import lax
from jax.experimental import pallas as pl
from jax.experimental.pallas import tpu as pltpu
from jax.sharding import PartitionSpec as P

TILE = 128
ITERS = 4
ROUNDS = 2

primal_step = 0.9
dual_step = 0.9
penalty = 1.0

MESH = pl.DeviceIdType.MESH
NX, NY, NC = 8, 8, 2
NZ = 8
NG = NX * NC
NN = (((1,), (0,)), ((), ()))
NT = (((1,), (1,)), ((), ()))


def dot(left, right, dims):
    return lax.dot_general(left, right, dims, preferred_element_type=jnp.float32)


def thirds(value):
    high = value.astype(jnp.bfloat16).astype(jnp.float32)
    rest = value - high
    middle = rest.astype(jnp.bfloat16).astype(jnp.float32)
    low = rest - middle
    return jnp.concatenate([high, middle, low], axis=0).astype(jnp.bfloat16)


def joined(rows):
    return (rows[0:1] + rows[1:2]) + rows[2:3]


def kernel(
    incidence,
    weights,
    coupling,
    cost_ref,
    capacity_ref,
    demand_ref,
    slots_ref,
    flows_out,
    duals_out,
    multipliers_out,
    consensus_out,
    spread_out,
    masked,
    pick,
    loads,
    group,
    plane,
    squares,
    duals_ref,
    copy_sem,
    load_send,
    load_recv,
    group_send,
    group_recv,
    plane_send,
    plane_recv,
    square_send,
    square_recv,
):
    scen = lax.axis_index("scen")
    z = lax.axis_index("arc")
    x = scen // (NY * NC)
    y = (scen // NC) % NY
    core = scen % NC
    mine = x * NC + core

    def z_partner(step):
        return (scen, lax.rem(z + step, NZ))

    def group_partner(step):
        other = lax.rem(mine + step, NG)
        return ((other // NC * NY + y) * NC + other % NC, z)

    def plane_partner(step):
        return ((x * NY + lax.rem(y + step, NY)) * NC + core, z)

    barrier = pltpu.get_barrier_semaphore()
    for step in range(1, NZ):
        pl.semaphore_signal(barrier, inc=1, device_id=z_partner(step), device_id_type=MESH)
    for step in range(1, NG):
        pl.semaphore_signal(barrier, inc=1, device_id=group_partner(step), device_id_type=MESH)
    for step in range(1, NY):
        pl.semaphore_signal(barrier, inc=1, device_id=plane_partner(step), device_id_type=MESH)

    blocks = coupling.shape[0] // TILE
    arcs = coupling.shape[1]
    fetch = pltpu.make_async_copy(coupling, masked, copy_sem)
    fetch.start()

    cost = cost_ref[...]
    capacity = capacity_ref[...]
    demand = demand_ref[...]
    slots = slots_ref[...]
    fleets = slots.shape[1]
    places = lax.broadcasted_iota(jnp.int32, (arcs, fleets), 0)
    pick[...] = jnp.where(places == slots, 1.0, 0.0).astype(jnp.bfloat16)
    is_fleet = dot(jnp.ones((1, fleets), jnp.bfloat16), pick[...], NT) > 0.5
    share = jnp.full((1, fleets), weights[0].astype(jnp.float32))

    fetch.wait()
    for row in range(blocks):
        for column in range(arcs // TILE):
            tile = (pl.ds(row * TILE, TILE), pl.ds(column * TILE, TILE))
            factor = incidence[row, column].astype(jnp.float32)
            masked[tile] = masked[tile] * jnp.full((TILE, TILE), factor, jnp.float32).astype(jnp.bfloat16)

    def send_all(buffer, own, partner, count, send_sem, recv_sem):
        for step in range(1, count):
            pltpu.make_async_remote_copy(
                src_ref=buffer.at[own],
                dst_ref=buffer.at[own],
                send_sem=send_sem,
                recv_sem=recv_sem,
                device_id=partner(step),
                device_id_type=MESH,
            ).start()

    def others(buffer, partner, count, send_sem, recv_sem):
        rest = buffer.at[pl.ds(0, count - 1)]
        return pltpu.make_async_remote_copy(
            src_ref=rest,
            dst_ref=rest,
            send_sem=send_sem,
            recv_sem=recv_sem,
            device_id=partner(1),
            device_id_type=MESH,
        )

    flows = jnp.zeros((1, arcs), jnp.float32)
    duals = jnp.zeros(demand.shape, jnp.float32)
    multipliers = jnp.zeros((1, fleets), jnp.float32)
    arc_multipliers = jnp.zeros((1, arcs), jnp.float32)
    arc_consensus = jnp.zeros((1, arcs), jnp.float32)
    pending = []
    deviations = []
    for round_index in range(ROUNDS):
        for step_index in range(ITERS):
            turn = round_index * ITERS + step_index
            gradient = cost
            if turn > 0:
                row = jnp.concatenate([duals[i : i + 1] for i in range(blocks)], axis=1)
                gradient = cost + dot(row.astype(jnp.bfloat16), masked[...], NN)
                if step_index == 0:
                    last = round_index - 1
                    wait = others(plane.at[last], plane_partner, NY, plane_send.at[last], plane_recv.at[last])
                    wait.wait_recv()
                    pending.append(wait)
                    consensus, weight_sum, square = settle(plane.at[last])
                    deviations.append(square)
                    multipliers = multipliers + penalty * (fleet_flow - consensus)
                    arc_consensus = joined(dot(thirds(consensus), pick[...], NT))
                    arc_multipliers = arc_multipliers + penalty * jnp.where(is_fleet, flows - arc_consensus, 0.0)
                push = arc_multipliers + penalty * (flows - arc_consensus)
                gradient = gradient + jnp.where(is_fleet, push, 0.0)
            flows_next = jnp.clip(flows - primal_step * gradient, 0.0, capacity)
            flows_bar = (2.0 * flows_next - flows).astype(jnp.bfloat16)
            flows = flows_next
            if turn == 0:
                pl.semaphore_wait(barrier, NZ + NG + NY - 3)
            if step_index == ITERS - 1:
                fleet_flow = joined(dot(thirds(flows), pick[...], NN))
                heap = group.at[round_index]
                heap[mine] = jnp.concatenate([fleet_flow, share], axis=0)
                send_all(heap, mine, group_partner, NG, group_send.at[round_index], group_recv.at[round_index])
            load = dot(flows_bar, masked[...], NT)
            heap = loads.at[turn]
            for i in range(blocks):
                heap[z, i : i + 1, :] = load[:, i * TILE : (i + 1) * TILE]
            send_all(heap, z, z_partner, NZ, load_send.at[turn], load_recv.at[turn])
            if step_index == ITERS - 1:
                heap = group.at[round_index]
                wait = others(heap, group_partner, NG, group_send.at[round_index], group_recv.at[round_index])
                wait.wait_recv()
                pending.append(wait)
                total = jnp.zeros((1, fleets), jnp.float32)
                weight = jnp.zeros((1, fleets), jnp.float32)
                for i in range(NG):
                    total = total + heap[i, 1:2] * heap[i, 0:1]
                    weight = weight + heap[i, 1:2]
                mean = total / weight
                square = jnp.zeros((1, fleets), jnp.float32)
                for i in range(NG):
                    gap = heap[i, 0:1] - mean
                    square = square + heap[i, 1:2] * gap * gap
                heap = plane.at[round_index]
                heap[y] = jnp.concatenate([total, weight, mean, square], axis=0)
                send_all(heap, y, plane_partner, NY, plane_send.at[round_index], plane_recv.at[round_index])
            heap = loads.at[turn]
            wait = others(heap, z_partner, NZ, load_send.at[turn], load_recv.at[turn])
            wait.wait_recv()
            pending.append(wait)
            row_load = heap[0]
            for i in range(1, NZ):
                row_load = row_load + heap[i]
            duals = jnp.maximum(duals + dual_step * (row_load - demand), 0.0)

    flows_out[...] = flows
    duals_ref[...] = duals
    duals_out[...] = duals_ref[pl.ds(z, 1), :]

    last = ROUNDS - 1
    wait = others(plane.at[last], plane_partner, NY, plane_send.at[last], plane_recv.at[last])
    wait.wait_recv()
    pending.append(wait)
    consensus, weight_sum, square = settle(plane.at[last])
    deviations.append(square)
    squares[z] = jnp.concatenate(deviations, axis=0)
    send_all(squares, z, z_partner, NZ, square_send, square_recv)
    consensus_out[...] = consensus
    multipliers_out[...] = multipliers + penalty * (fleet_flow - consensus)
    wait = others(squares, z_partner, NZ, square_send, square_recv)
    wait.wait_recv()
    pending.append(wait)
    total = squares[0]
    for i in range(1, NZ):
        total = total + squares[i]
    total = jnp.sum(total, axis=1, keepdims=True)
    spread_out[...] = jnp.sqrt(total / (weight_sum[:, 0:1] * (fleets * NZ)) + 1e-06)
    for wait in pending:
        wait.wait_send()


def settle(heap):
    total = heap[0, 0:1]
    weight = heap[0, 1:2]
    for i in range(1, NY):
        total = total + heap[i, 0:1]
        weight = weight + heap[i, 1:2]
    consensus = total / weight
    square = jnp.zeros_like(total)
    for i in range(NY):
        gap = heap[i, 2:3] - consensus
        square = square + (heap[i, 3:4] + heap[i, 1:2] * gap * gap)
    return consensus, weight, square


def body(coupling, incidence, arc_cost, capacity, demand, weights, fleet_slots):
    rows, arcs = coupling.shape
    fleets = fleet_slots.shape[0]
    turns = ROUNDS * ITERS
    f32 = jnp.float32
    vmem = pl.BlockSpec(memory_space=pltpu.VMEM)
    smem = pl.BlockSpec(memory_space=pltpu.SMEM)
    flows, duals, multipliers, consensus, spread = pl.pallas_call(
        kernel,
        out_shape=[
            jax.ShapeDtypeStruct((1, arcs), f32),
            jax.ShapeDtypeStruct((1, rows // NZ), f32),
            jax.ShapeDtypeStruct((1, fleets), f32),
            jax.ShapeDtypeStruct((1, fleets), f32),
            jax.ShapeDtypeStruct((ROUNDS, 1), f32),
        ],
        in_specs=[smem, smem, pl.BlockSpec(memory_space=pl.ANY)] + [vmem] * 4,
        out_specs=[vmem] * 5,
        scratch_shapes=[
            pltpu.VMEM((rows, arcs), jnp.bfloat16),
            pltpu.VMEM((arcs, fleets), jnp.bfloat16),
            pltpu.VMEM((turns, NZ, rows // TILE, TILE), f32),
            pltpu.VMEM((ROUNDS, NG, 2, fleets), f32),
            pltpu.VMEM((ROUNDS, NY, 4, fleets), f32),
            pltpu.VMEM((NZ, ROUNDS, fleets), f32),
            pltpu.VMEM((rows // TILE, TILE), f32),
            pltpu.SemaphoreType.DMA,
            pltpu.SemaphoreType.DMA((turns,)),
            pltpu.SemaphoreType.DMA((turns,)),
            pltpu.SemaphoreType.DMA((ROUNDS,)),
            pltpu.SemaphoreType.DMA((ROUNDS,)),
            pltpu.SemaphoreType.DMA((ROUNDS,)),
            pltpu.SemaphoreType.DMA((ROUNDS,)),
            pltpu.SemaphoreType.DMA,
            pltpu.SemaphoreType.DMA,
        ],
        compiler_params=pltpu.CompilerParams(
            collective_id=0, has_side_effects=True, vmem_limit_bytes=16 * 1024 * 1024
        ),
        cost_estimate=pl.CostEstimate(
            flops=4 * turns * rows * arcs, bytes_accessed=2 * rows * arcs, transcendentals=0
        ),
    )(
        incidence,
        weights,
        coupling,
        arc_cost.reshape(1, arcs),
        capacity.reshape(1, arcs),
        demand.reshape(rows // TILE, TILE),
        fleet_slots.reshape(1, fleets),
    )
    return flows, duals, multipliers, consensus.reshape(fleets), spread.reshape(ROUNDS)


def solution(mesh):
    in_specs = (
        P(None, "arc"),
        P(None, "arc"),
        P("arc"),
        P("arc"),
        P("scen", None),
        P("scen"),
        P("arc"),
    )
    out_specs = (P("scen", "arc"), P("scen", "arc"), P("scen", "arc"), P("arc"), P())
    return jax.shard_map(body, mesh=mesh, in_specs=in_specs, out_specs=out_specs, check_vma=False)
```

```python
import jax
import jax.numpy as jnp
from jax import lax
from jax.experimental import pallas as pl
from jax.experimental.pallas import tpu as pltpu
from jax.sharding import PartitionSpec as P

TILE = 128
ITERS = 4
ROUNDS = 2

primal_step = 0.9
dual_step = 0.9
penalty = 1.0

MESH = pl.DeviceIdType.MESH
NX, NY, NC, NZ = 8, 8, 2, 8
NG = NX * NC
SCEN = NG * NY
CHUNKS = 4
NN = (((1,), (0,)), ((), ()))
NT = (((1,), (1,)), ((), ()))


def dot(left, right, dims):
    return lax.dot_general(left, right, dims, preferred_element_type=jnp.float32)


def thirds(value):
    high = value.astype(jnp.bfloat16).astype(jnp.float32)
    rest = value - high
    middle = rest.astype(jnp.bfloat16).astype(jnp.float32)
    low = rest - middle
    return jnp.concatenate([high, middle, low], axis=0).astype(jnp.bfloat16)


def joined(rows):
    return (rows[0:1] + rows[1:2]) + rows[2:3]


def far(size):
    return sorted(range(size), key=lambda step: -min(step, size - step))


def hops(step, size):
    return min(step, size - step)


def kernel(
    coupling_hbm,
    incidence_hbm,
    cost_hbm,
    capacity_hbm,
    demand_hbm,
    weights_hbm,
    slots_hbm,
    flows_out,
    duals_out,
    multipliers_out,
    consensus_out,
    spread_out,
    flows_ref,
    duals_ref,
    multipliers_ref,
    consensus_ref,
    spread_ref,
    incidence,
    weights,
    cost_ref,
    capacity_ref,
    demand_ref,
    slots_ref,
    masked,
    turned,
    pick,
    loads,
    shares,
    fleet,
    squares,
    all_duals,
    fetch_sem,
    store_sem,
    load_send,
    load_recv,
    share_send,
    share_recv,
    fleet_send,
    fleet_recv,
    square_send,
    square_recv,
):
    scen = lax.axis_index("scen")
    z = lax.axis_index("arc")
    x = scen // (NY * NC)
    y = (scen // NC) % NY
    core = scen % NC
    mine = y * NG + x * NC + core

    def at(dx, dy, dc):
        other = (lax.rem(x + dx, NX) * NY + lax.rem(y + dy, NY)) * NC + lax.rem(core + dc, NC)
        return (other, z)

    along_z = [(scen, lax.rem(z + step, NZ)) for step in far(NZ)[:-1]]
    group = [at(dx, 0, dc) for dx in far(NX) for dc in (1, 0) if dx + dc > 0]
    plane = [at(0, dy, 0) for dy in far(NY)[:-1]]
    steps = [(dx, dy, dc) for dx in range(NX) for dy in range(NY) for dc in range(NC)]
    steps = [s for s in steps if s != (0, 0, 0)]
    steps.sort(key=lambda s: -hops(s[0], NX) - hops(s[1], NY))

    barrier = pltpu.get_barrier_semaphore()
    greeted = along_z + group + plane
    for other in greeted:
        pl.semaphore_signal(barrier, inc=1, device_id=other, device_id_type=MESH)

    rows, arcs = masked.shape
    blocks = rows // TILE
    fleets = slots_ref.shape[1]
    depth = rows // CHUNKS
    fetches = []

    def fetch(source, target):
        copy = pltpu.make_async_copy(source, target, fetch_sem.at[len(fetches)])
        copy.start()
        fetches.append(copy)
        return copy

    fetch_incidence = fetch(incidence_hbm, incidence)
    fetch_cost = fetch(cost_hbm, cost_ref)
    fetch_capacity = fetch(capacity_hbm, capacity_ref)
    parts = [pl.ds(chunk * depth, depth) for chunk in range(CHUNKS)]
    fetch_masked = [fetch(coupling_hbm.at[part], masked.at[part]) for part in parts]
    fetch_slots = fetch(slots_hbm, slots_ref)
    fetch_demand = fetch(demand_hbm, demand_ref)
    fetch_weights = fetch(weights_hbm, weights)

    def store(index, source, target):
        copy = pltpu.make_async_copy(source, target, store_sem.at[index])
        copy.start()
        return copy

    def send(source, target, partner, send_sem, recv_sem):
        pltpu.make_async_remote_copy(
            src_ref=source,
            dst_ref=target,
            send_sem=send_sem,
            recv_sem=recv_sem,
            device_id=partner,
            device_id_type=MESH,
        ).start()

    def awaited(rest, send_sem, recv_sem):
        return pltpu.make_async_remote_copy(
            src_ref=rest,
            dst_ref=rest,
            send_sem=send_sem,
            recv_sem=recv_sem,
            device_id=along_z[0],
            device_id_type=MESH,
        )

    def exchange(buffer, send_sem, recv_sem):
        for partner in along_z:
            send(buffer.at[z], buffer.at[z], partner, send_sem, recv_sem)
        return awaited(buffer.at[pl.ds(0, NZ - 1)], send_sem, recv_sem)

    fetch_cost.wait()
    fetch_capacity.wait()
    cost = cost_ref[...]
    capacity = capacity_ref[...]
    flows = jnp.clip(-primal_step * cost, 0.0, capacity)
    flows_bar = (2.0 * flows).astype(jnp.bfloat16)
    fetch_incidence.wait()
    for chunk, part in enumerate(parts):
        fetch_masked[chunk].wait()
        for row in range(chunk * depth // TILE, (chunk + 1) * depth // TILE):
            for column in range(arcs // TILE):
                tile = (pl.ds(row * TILE, TILE), pl.ds(column * TILE, TILE))
                factor = incidence[column, row].astype(jnp.float32)
                masked[tile] = masked[tile] * jnp.full((TILE, TILE), factor, jnp.float32).astype(jnp.bfloat16)
        load = dot(flows_bar, masked[part], NT)
        for i in range(depth // TILE):
            loads[0, z, pl.ds(chunk * depth // TILE + i, 1), :] = load[:, i * TILE : (i + 1) * TILE]
    pl.semaphore_wait(barrier, len(greeted))
    waits = [exchange(loads.at[0], load_send.at[0], load_recv.at[0])]

    fetch_weights.wait()
    own_row = pl.ds(mine, 1)
    shares[own_row, :] = jnp.full((1, fleets), weights[0].astype(jnp.float32))
    for partner in group:
        send(shares.at[own_row], shares.at[own_row], partner, share_send.at[0], share_recv.at[0])
    share_group = awaited(shares.at[pl.ds(0, NG - 1)], share_send.at[0], share_recv.at[0])
    for part in parts:
        turned[:, part] = masked[part].T
    fetch_slots.wait()
    places = lax.broadcasted_iota(jnp.int32, (arcs, fleets), 0)
    pick[...] = jnp.where(places == slots_ref[...], 1.0, 0.0).astype(jnp.bfloat16)
    is_fleet = dot(jnp.ones((1, fleets), jnp.bfloat16), pick[...], NT) > 0.5
    fetch_demand.wait()
    demand = demand_ref[...]

    def next_duals(duals, turn):
        waits[turn].wait_recv()
        row_load = loads[turn, 0]
        for i in range(1, NZ):
            row_load = row_load + loads[turn, i]
        return jnp.maximum(duals + dual_step * (row_load - demand), 0.0)

    duals = next_duals(jnp.zeros(demand.shape, jnp.float32), 0)
    multipliers = jnp.zeros((1, fleets), jnp.float32)
    arc_multipliers = jnp.zeros((1, arcs), jnp.float32)
    arc_consensus = jnp.zeros((1, arcs), jnp.float32)
    deviations = []
    pending = []
    for turn in range(1, ROUNDS * ITERS):
        row = jnp.concatenate([duals[i : i + 1] for i in range(blocks)], axis=1)
        gradient = cost + dot(row.astype(jnp.bfloat16), masked[...], NN)
        push = arc_multipliers + penalty * (flows - arc_consensus)
        gradient = gradient + jnp.where(is_fleet, push, 0.0)
        flows_next = jnp.clip(flows - primal_step * gradient, 0.0, capacity)
        flows_bar = (2.0 * flows_next - flows).astype(jnp.bfloat16)
        flows = flows_next
        round_index = turn // ITERS
        round_ends = turn % ITERS == ITERS - 1
        if round_ends:
            fleet_flow = joined(dot(thirds(flows), pick[...], NN))
            heap = fleet.at[round_index]
            fleet[round_index, own_row, :] = fleet_flow
            for step in steps:
                send(
                    heap.at[own_row],
                    heap.at[own_row],
                    at(*step),
                    fleet_send.at[round_index],
                    fleet_recv.at[round_index],
                )
            arrival = awaited(
                heap.at[pl.ds(0, SCEN - 1)], fleet_send.at[round_index], fleet_recv.at[round_index]
            )
        load = dot(flows_bar, turned[...], NN)
        for i in range(blocks):
            loads[turn, z, i : i + 1, :] = load[:, i * TILE : (i + 1) * TILE]
        waits.append(exchange(loads.at[turn], load_send.at[turn], load_recv.at[turn]))
        if turn == 1:
            share_group.wait_recv()
            own_rows = pl.ds(pl.multiple_of(y * NG, NG), NG)
            for partner in plane:
                send(shares.at[own_rows], shares.at[own_rows], partner, share_send.at[1], share_recv.at[1])
            share_plane = awaited(shares.at[pl.ds(0, SCEN - NG)], share_send.at[1], share_recv.at[1])
        if turn == 2:
            share_plane.wait_recv()
            pending += [share_group, share_plane]
            weight_sum = jnp.sum(shares[...], axis=0, keepdims=True)
        duals = next_duals(duals, turn)
        if round_ends:
            if turn == ROUNDS * ITERS - 1:
                flows_ref[...] = flows
                all_duals[...] = duals
                duals_ref[...] = all_duals[pl.ds(z, 1), :]
                stores = [store(0, flows_ref, flows_out), store(1, duals_ref, duals_out)]
            arrival.wait_recv()
            pending.append(arrival)
            all_fleet = heap[...]
            consensus = jnp.sum(shares[...] * all_fleet, axis=0, keepdims=True) / weight_sum
            gap = all_fleet - consensus
            deviations.append(jnp.sum(shares[...] * gap * gap, axis=0, keepdims=True))
            multipliers = multipliers + penalty * (fleet_flow - consensus)
            if turn < ROUNDS * ITERS - 1:
                arc_consensus = joined(dot(thirds(consensus), pick[...], NT))
                arc_multipliers = arc_multipliers + penalty * jnp.where(is_fleet, flows - arc_consensus, 0.0)

    squares[z] = jnp.concatenate(deviations, axis=0)
    wait = exchange(squares, square_send, square_recv)
    multipliers_ref[...] = multipliers
    consensus_ref[...] = consensus
    stores += [store(2, multipliers_ref, multipliers_out), store(3, consensus_ref, consensus_out)]
    for done in waits + pending:
        done.wait_send()
    wait.wait_recv()
    total = squares[0]
    for i in range(1, NZ):
        total = total + squares[i]
    total = jnp.sum(total, axis=1, keepdims=True)
    spread = jnp.sqrt(total / (weight_sum[:, 0:1] * (fleets * NZ)) + 1e-06)
    spread_ref[...] = jnp.concatenate([spread[i : i + 1] for i in range(ROUNDS)], axis=1)
    stores.append(store(4, spread_ref, spread_out))
    wait.wait_send()
    for done in stores:
        done.wait()


def place(*refs):
    count = len(refs) // 2
    sem = refs[-1]
    copies = [pltpu.make_async_copy(refs[i], refs[count + i], sem.at[i]) for i in range(count)]
    for copy in copies:
        copy.start()
    for copy in copies:
        copy.wait()


def body(coupling, incidence, arc_cost, capacity, demand, weights, fleet_slots):
    rows, arcs = coupling.shape
    fleets = fleet_slots.shape[0]
    turns = ROUNDS * ITERS
    f32 = jnp.float32
    hbm = pl.BlockSpec(memory_space=pltpu.HBM)
    dma = pltpu.SemaphoreType.DMA
    outs = [
        jax.ShapeDtypeStruct((1, arcs), f32),
        jax.ShapeDtypeStruct((1, rows // NZ), f32),
        jax.ShapeDtypeStruct((1, fleets), f32),
        jax.ShapeDtypeStruct((1, fleets), f32),
        jax.ShapeDtypeStruct((1, ROUNDS), f32),
    ]
    results = pl.pallas_call(
        kernel,
        out_shape=outs,
        in_specs=[hbm] * 7,
        out_specs=[hbm] * 5,
        scratch_shapes=[
            pltpu.VMEM((1, arcs), f32),
            pltpu.VMEM((1, rows // NZ), f32),
            pltpu.VMEM((1, fleets), f32),
            pltpu.VMEM((1, fleets), f32),
            pltpu.VMEM((1, ROUNDS), f32),
            pltpu.SMEM((arcs // TILE, rows // TILE), jnp.int32),
            pltpu.SMEM((1,), jnp.int32),
            pltpu.VMEM((1, arcs), f32),
            pltpu.VMEM((1, arcs), f32),
            pltpu.VMEM((rows // TILE, TILE), f32),
            pltpu.VMEM((1, fleets), jnp.int32),
            pltpu.VMEM((rows, arcs), jnp.bfloat16),
            pltpu.VMEM((arcs, rows), jnp.bfloat16),
            pltpu.VMEM((arcs, fleets), jnp.bfloat16),
            pltpu.VMEM((turns, NZ, rows // TILE, TILE), f32),
            pltpu.VMEM((SCEN, fleets), f32),
            pltpu.VMEM((ROUNDS, SCEN, fleets), f32),
            pltpu.VMEM((NZ, ROUNDS, fleets), f32),
            pltpu.VMEM((rows // TILE, TILE), f32),
            dma((6 + CHUNKS,)),
            dma((5,)),
            dma((turns,)),
            dma((turns,)),
            dma((2,)),
            dma((2,)),
            dma((ROUNDS,)),
            dma((ROUNDS,)),
            dma,
            dma,
        ],
        compiler_params=pltpu.CompilerParams(
            collective_id=0, has_side_effects=True, vmem_limit_bytes=60 * 1024 * 1024
        ),
        cost_estimate=pl.CostEstimate(
            flops=4 * turns * rows * arcs, bytes_accessed=2 * rows * arcs, transcendentals=0
        ),
    )(
        coupling,
        incidence.T,
        arc_cost.reshape(1, arcs),
        capacity.reshape(1, arcs),
        demand.reshape(rows // TILE, TILE),
        weights,
        fleet_slots.reshape(1, fleets),
    )
    flows, duals, multipliers, consensus, spread = pl.pallas_call(
        place,
        out_shape=outs,
        in_specs=[hbm] * 5,
        out_specs=[hbm] * 5,
        scratch_shapes=[dma((5,))],
    )(*results)
    return flows, duals, multipliers, consensus.reshape(fleets), spread.reshape(ROUNDS)


def solution(mesh):
    in_specs = (
        P(None, "arc"),
        P(None, "arc"),
        P("arc"),
        P("arc"),
        P("scen", None),
        P("scen"),
        P("arc"),
    )
    out_specs = (P("scen", "arc"), P("scen", "arc"), P("scen", "arc"), P("arc"), P())
    return jax.shard_map(body, mesh=mesh, in_specs=in_specs, out_specs=out_specs, check_vma=False)
```

```python
import jax
import jax.numpy as jnp
from jax import lax
from jax.experimental import pallas as pl
from jax.experimental.pallas import tpu as pltpu
from jax.sharding import PartitionSpec as P

TILE = 128
ITERS = 4
ROUNDS = 2

primal_step = 0.9
dual_step = 0.9
penalty = 1.0

MESH = pl.DeviceIdType.MESH
NX, NY, NC, NZ = 8, 8, 2, 8
NG = NX * NC
SCEN = NG * NY
CHUNKS = 4
EARLY = 26
NN = (((1,), (0,)), ((), ()))
NT = (((1,), (1,)), ((), ()))


def dot(left, right, dims):
    return lax.dot_general(left, right, dims, preferred_element_type=jnp.float32)


def thirds(value):
    high = value.astype(jnp.bfloat16).astype(jnp.float32)
    rest = value - high
    middle = rest.astype(jnp.bfloat16).astype(jnp.float32)
    low = rest - middle
    return jnp.concatenate([high, middle, low], axis=0).astype(jnp.bfloat16)


def joined(rows):
    return (rows[0:1] + rows[1:2]) + rows[2:3]


def far(size):
    return sorted(range(size), key=lambda step: -min(step, size - step))


def hops(step, size):
    return min(step, size - step)


def kernel(
    coupling_hbm,
    incidence_hbm,
    cost_hbm,
    capacity_hbm,
    demand_hbm,
    weights_hbm,
    slots_hbm,
    flows_out,
    duals_out,
    multipliers_out,
    consensus_out,
    spread_out,
    flows_ref,
    duals_ref,
    multipliers_ref,
    consensus_ref,
    spread_ref,
    incidence,
    weights,
    cost_ref,
    capacity_ref,
    demand_ref,
    slots_ref,
    masked,
    turned,
    pick,
    fleet_columns,
    fleet_rows,
    loads,
    shares,
    fleet,
    squares,
    all_duals,
    fetch_sem,
    store_sem,
    load_send,
    load_recv,
    share_send,
    share_recv,
    fleet_send,
    fleet_recv,
    square_send,
    square_recv,
):
    scen = lax.axis_index("scen")
    z = lax.axis_index("arc")
    x = scen // (NY * NC)
    y = (scen // NC) % NY
    core = scen % NC
    mine = y * NG + x * NC + core

    def at(dx, dy, dc):
        other = (lax.rem(x + dx, NX) * NY + lax.rem(y + dy, NY)) * NC + lax.rem(core + dc, NC)
        return (other, z)

    along_z = [(scen, lax.rem(z + step, NZ)) for step in far(NZ)[:-1]]
    group_steps = [(dx, 0, dc) for dx in far(NX) for dc in (1, 0) if dx + dc > 0]
    plane_steps = [(0, dy, 0) for dy in far(NY)[:-1]]
    group = [at(*step) for step in group_steps]
    plane = [at(*step) for step in plane_steps]
    steps = [(dx, dy, dc) for dx in range(NX) for dy in range(NY) for dc in range(NC)]
    steps = [s for s in steps if s != (0, 0, 0)]
    steps.sort(key=lambda s: -hops(s[0], NX) - hops(s[1], NY))

    barrier = pltpu.get_barrier_semaphore()
    greeted = [(hops(step, NZ), other) for step, other in zip(far(NZ), along_z)]
    greeted += [(hops(step[0], NX), other) for step, other in zip(group_steps, group)]
    greeted += [(hops(step[1], NY), other) for step, other in zip(plane_steps, plane)]
    greeted.sort(key=lambda entry: -entry[0])
    for _, other in greeted:
        pl.semaphore_signal(barrier, inc=1, device_id=other, device_id_type=MESH)

    rows, arcs = masked.shape
    blocks = rows // TILE
    fleets = slots_ref.shape[1]
    depth = rows // CHUNKS
    fetches = []

    def fetch(source, target):
        copy = pltpu.make_async_copy(source, target, fetch_sem.at[len(fetches)])
        copy.start()
        fetches.append(copy)
        return copy

    fetch_incidence = fetch(incidence_hbm, incidence)
    fetch_cost = fetch(cost_hbm, cost_ref)
    fetch_capacity = fetch(capacity_hbm, capacity_ref)
    parts = [pl.ds(chunk * depth, depth) for chunk in range(CHUNKS)]
    fetch_masked = [fetch(coupling_hbm.at[part], masked.at[part]) for part in parts]
    fetch_slots = fetch(slots_hbm, slots_ref)
    fetch_demand = fetch(demand_hbm, demand_ref)
    fetch_weights = fetch(weights_hbm, weights)

    def store(index, source, target):
        copy = pltpu.make_async_copy(source, target, store_sem.at[index])
        copy.start()
        return copy

    def send(source, target, partner, send_sem, recv_sem):
        pltpu.make_async_remote_copy(
            src_ref=source,
            dst_ref=target,
            send_sem=send_sem,
            recv_sem=recv_sem,
            device_id=partner,
            device_id_type=MESH,
        ).start()

    def awaited(rest, send_sem, recv_sem):
        return pltpu.make_async_remote_copy(
            src_ref=rest,
            dst_ref=rest,
            send_sem=send_sem,
            recv_sem=recv_sem,
            device_id=along_z[0],
            device_id_type=MESH,
        )

    def exchange(buffer, send_sem, recv_sem):
        for partner in along_z:
            send(buffer.at[z], buffer.at[z], partner, send_sem, recv_sem)
        return awaited(buffer.at[pl.ds(0, NZ - 1)], send_sem, recv_sem)

    fetch_cost.wait()
    fetch_capacity.wait()
    cost = cost_ref[...]
    capacity = capacity_ref[...]
    flows = jnp.clip(-primal_step * cost, 0.0, capacity)
    flows_bar = (2.0 * flows).astype(jnp.bfloat16)
    fetch_incidence.wait()
    for chunk, part in enumerate(parts):
        fetch_masked[chunk].wait()
        for row in range(chunk * depth // TILE, (chunk + 1) * depth // TILE):
            for column in range(arcs // TILE):
                tile = (pl.ds(row * TILE, TILE), pl.ds(column * TILE, TILE))
                factor = incidence[column, row].astype(jnp.float32)
                masked[tile] = masked[tile] * jnp.full((TILE, TILE), factor, jnp.float32).astype(jnp.bfloat16)
        load = dot(flows_bar, masked[part], NT)
        for i in range(depth // TILE):
            loads[0, z, pl.ds(chunk * depth // TILE + i, 1), :] = load[:, i * TILE : (i + 1) * TILE]
    pl.semaphore_wait(barrier, len(greeted))
    waits = [exchange(loads.at[0], load_send.at[0], load_recv.at[0])]

    fetch_weights.wait()
    own_row = pl.ds(mine, 1)
    shares[own_row, :] = jnp.full((1, fleets), weights[0].astype(jnp.float32))
    for partner in group:
        send(shares.at[own_row], shares.at[own_row], partner, share_send.at[0], share_recv.at[0])
    share_group = awaited(shares.at[pl.ds(0, NG - 1)], share_send.at[0], share_recv.at[0])
    for part in parts:
        turned[:, part] = masked[part].T
    fetch_slots.wait()
    places = lax.broadcasted_iota(jnp.int32, (arcs, fleets), 0)
    pick[...] = jnp.where(places == slots_ref[...], 1.0, 0.0).astype(jnp.bfloat16)
    is_fleet = dot(jnp.ones((1, fleets), jnp.bfloat16), pick[...], NT) > 0.5
    fetch_demand.wait()
    demand = demand_ref[...]

    def gathered(value):
        return joined(dot(thirds(value), pick[...], NN))

    def on_arcs(value):
        return joined(dot(thirds(value), pick[...], NT))

    def send_fleet(round_index, some_steps):
        line = fleet.at[round_index, own_row]
        for step in some_steps:
            send(line, line, at(*step), fleet_send.at[round_index], fleet_recv.at[round_index])

    def settle(round_index):
        arrival = awaited(
            fleet.at[round_index, pl.ds(0, SCEN - 1)], fleet_send.at[round_index], fleet_recv.at[round_index]
        )
        arrival.wait_recv()
        pending.append(arrival)
        return jnp.sum(shares[...] * fleet[round_index], axis=0, keepdims=True) / weight_sum

    def deviation(round_index, consensus):
        gap = fleet[round_index] - consensus
        return jnp.sum(shares[...] * gap * gap, axis=0, keepdims=True)

    def next_duals(duals, turn):
        waits[turn].wait_recv()
        row_load = loads[turn, 0]
        for i in range(1, NZ):
            row_load = row_load + loads[turn, i]
        return jnp.maximum(duals + dual_step * (row_load - demand), 0.0)

    fleet_columns[...] = dot(masked[...], pick[...], NN).astype(jnp.bfloat16)
    fleet_rows[...] = fleet_columns[...].T
    fleet_cost = gathered(cost)
    fleet_capacity = gathered(capacity)

    last_turn = ROUNDS * ITERS - 1
    duals = next_duals(jnp.zeros(demand.shape, jnp.float32), 0)
    multipliers = jnp.zeros((1, fleets), jnp.float32)
    consensus = jnp.zeros((1, fleets), jnp.float32)
    arc_multipliers = jnp.zeros((1, arcs), jnp.float32)
    arc_consensus = jnp.zeros((1, arcs), jnp.float32)
    deviations = []
    pending = []
    for turn in range(1, ROUNDS * ITERS):
        round_index = turn // ITERS
        row = jnp.concatenate([duals[i : i + 1] for i in range(blocks)], axis=1).astype(jnp.bfloat16)
        round_starts = turn % ITERS == 0
        round_ends = turn % ITERS == ITERS - 1
        later = []
        if round_starts or round_ends:
            fleet_gradient = fleet_cost + dot(row, fleet_columns[...], NN)
        if round_ends:
            fleet_gradient = fleet_gradient + (multipliers + penalty * (fleet_flow - consensus))
            fleet_flow = jnp.clip(fleet_flow - primal_step * fleet_gradient, 0.0, fleet_capacity)
            fleet[round_index, own_row, :] = fleet_flow
            early = len(steps) if turn == last_turn else EARLY
            send_fleet(round_index, steps[:early])
            later = steps[early:]
        gradient = cost + dot(row, masked[...], NN)
        if round_starts:
            flows_next = jnp.clip(flows - primal_step * gradient, 0.0, capacity)
            flows_bar = jnp.where(is_fleet, 0.0, 2.0 * flows_next - flows).astype(jnp.bfloat16)
            load = dot(flows_bar, turned[...], NN)
            consensus = settle(round_index - 1)
            multipliers = multipliers + penalty * (fleet_flow - consensus)
            fleet_gradient = fleet_gradient + (multipliers + penalty * (fleet_flow - consensus))
            fleet_next = jnp.clip(fleet_flow - primal_step * fleet_gradient, 0.0, fleet_capacity)
            fleet_bar = (2.0 * fleet_next - fleet_flow).astype(jnp.bfloat16)
            load = load + dot(fleet_bar, fleet_rows[...], NN)
        else:
            push = arc_multipliers + penalty * (flows - arc_consensus)
            gradient = gradient + jnp.where(is_fleet, push, 0.0)
            flows_next = jnp.clip(flows - primal_step * gradient, 0.0, capacity)
            flows_bar = (2.0 * flows_next - flows).astype(jnp.bfloat16)
            load = dot(flows_bar, turned[...], NN)
        for i in range(blocks):
            loads[turn, z, i : i + 1, :] = load[:, i * TILE : (i + 1) * TILE]
        waits.append(exchange(loads.at[turn], load_send.at[turn], load_recv.at[turn]))
        send_fleet(round_index, later)
        if round_starts:
            flows_next = jnp.where(is_fleet, on_arcs(fleet_next), flows_next)
            arc_consensus = on_arcs(consensus)
            arc_multipliers = on_arcs(multipliers)
            deviations.append(deviation(round_index - 1, consensus))
        flows = flows_next
        if turn % ITERS == ITERS - 2:
            fleet_flow = gathered(flows)
        if turn == 1:
            share_group.wait_recv()
            own_rows = pl.ds(pl.multiple_of(y * NG, NG), NG)
            for partner in plane:
                send(shares.at[own_rows], shares.at[own_rows], partner, share_send.at[1], share_recv.at[1])
            share_plane = awaited(shares.at[pl.ds(0, SCEN - NG)], share_send.at[1], share_recv.at[1])
        if turn == 2:
            share_plane.wait_recv()
            pending += [share_group, share_plane]
            weight_sum = jnp.sum(shares[...], axis=0, keepdims=True)
        if turn < last_turn:
            duals = next_duals(duals, turn)

    consensus = settle(ROUNDS - 1)
    deviations.append(deviation(ROUNDS - 1, consensus))
    squares[z] = jnp.concatenate(deviations, axis=0)
    wait = exchange(squares, square_send, square_recv)
    multipliers_ref[...] = multipliers + penalty * (fleet_flow - consensus)
    consensus_ref[...] = consensus
    flows_ref[...] = flows
    all_duals[...] = next_duals(duals, last_turn)
    duals_ref[...] = all_duals[pl.ds(z, 1), :]
    stores = [
        store(0, flows_ref, flows_out),
        store(1, duals_ref, duals_out),
        store(2, multipliers_ref, multipliers_out),
        store(3, consensus_ref, consensus_out),
    ]
    for done in waits + pending:
        done.wait_send()
    wait.wait_recv()
    total = squares[0]
    for i in range(1, NZ):
        total = total + squares[i]
    total = jnp.sum(total, axis=1, keepdims=True)
    spread = jnp.sqrt(total / (weight_sum[:, 0:1] * (fleets * NZ)) + 1e-06)
    spread_ref[...] = jnp.concatenate([spread[i : i + 1] for i in range(ROUNDS)], axis=1)
    stores.append(store(4, spread_ref, spread_out))
    wait.wait_send()
    for done in stores:
        done.wait()


def place(*refs):
    count = len(refs) // 2
    sem = refs[-1]
    copies = [pltpu.make_async_copy(refs[i], refs[count + i], sem.at[i]) for i in range(count)]
    for copy in copies:
        copy.start()
    for copy in copies:
        copy.wait()


def body(coupling, incidence, arc_cost, capacity, demand, weights, fleet_slots):
    rows, arcs = coupling.shape
    fleets = fleet_slots.shape[0]
    turns = ROUNDS * ITERS
    f32 = jnp.float32
    hbm = pl.BlockSpec(memory_space=pltpu.HBM)
    dma = pltpu.SemaphoreType.DMA
    outs = [
        jax.ShapeDtypeStruct((1, arcs), f32),
        jax.ShapeDtypeStruct((1, rows // NZ), f32),
        jax.ShapeDtypeStruct((1, fleets), f32),
        jax.ShapeDtypeStruct((1, fleets), f32),
        jax.ShapeDtypeStruct((1, ROUNDS), f32),
    ]
    results = pl.pallas_call(
        kernel,
        out_shape=outs,
        in_specs=[hbm] * 7,
        out_specs=[hbm] * 5,
        scratch_shapes=[
            pltpu.VMEM((1, arcs), f32),
            pltpu.VMEM((1, rows // NZ), f32),
            pltpu.VMEM((1, fleets), f32),
            pltpu.VMEM((1, fleets), f32),
            pltpu.VMEM((1, ROUNDS), f32),
            pltpu.SMEM((arcs // TILE, rows // TILE), jnp.int32),
            pltpu.SMEM((1,), jnp.int32),
            pltpu.VMEM((1, arcs), f32),
            pltpu.VMEM((1, arcs), f32),
            pltpu.VMEM((rows // TILE, TILE), f32),
            pltpu.VMEM((1, fleets), jnp.int32),
            pltpu.VMEM((rows, arcs), jnp.bfloat16),
            pltpu.VMEM((arcs, rows), jnp.bfloat16),
            pltpu.VMEM((arcs, fleets), jnp.bfloat16),
            pltpu.VMEM((rows, fleets), jnp.bfloat16),
            pltpu.VMEM((fleets, rows), jnp.bfloat16),
            pltpu.VMEM((turns, NZ, rows // TILE, TILE), f32),
            pltpu.VMEM((SCEN, fleets), f32),
            pltpu.VMEM((ROUNDS, SCEN, fleets), f32),
            pltpu.VMEM((NZ, ROUNDS, fleets), f32),
            pltpu.VMEM((rows // TILE, TILE), f32),
            dma((6 + CHUNKS,)),
            dma((5,)),
            dma((turns,)),
            dma((turns,)),
            dma((2,)),
            dma((2,)),
            dma((ROUNDS,)),
            dma((ROUNDS,)),
            dma,
            dma,
        ],
        compiler_params=pltpu.CompilerParams(
            collective_id=0, has_side_effects=True, vmem_limit_bytes=60 * 1024 * 1024
        ),
        cost_estimate=pl.CostEstimate(
            flops=4 * turns * rows * arcs, bytes_accessed=2 * rows * arcs, transcendentals=0
        ),
    )(
        coupling,
        incidence.T,
        arc_cost.reshape(1, arcs),
        capacity.reshape(1, arcs),
        demand.reshape(rows // TILE, TILE),
        weights,
        fleet_slots.reshape(1, fleets),
    )
    flows, duals, multipliers, consensus, spread = pl.pallas_call(
        place,
        out_shape=outs,
        in_specs=[hbm] * 5,
        out_specs=[hbm] * 5,
        scratch_shapes=[dma((5,))],
    )(*results)
    return flows, duals, multipliers, consensus.reshape(fleets), spread.reshape(ROUNDS)


def solution(mesh):
    in_specs = (
        P(None, "arc"),
        P(None, "arc"),
        P("arc"),
        P("arc"),
        P("scen", None),
        P("scen"),
        P("arc"),
    )
    out_specs = (P("scen", "arc"), P("scen", "arc"), P("scen", "arc"), P("arc"), P())
    return jax.shard_map(body, mesh=mesh, in_specs=in_specs, out_specs=out_specs, check_vma=False)
```

```python
import jax
import jax.numpy as jnp
from jax import lax
from jax.experimental import pallas as pl
from jax.experimental.pallas import tpu as pltpu
from jax.sharding import PartitionSpec as P

TILE = 128
ITERS = 4
ROUNDS = 2

primal_step = 0.9
dual_step = 0.9
penalty = 1.0

MESH = pl.DeviceIdType.MESH
NX, NY, NC, NZ = 8, 8, 2, 8
NG = NX * NC
SCEN = NG * NY
CHUNKS = 4
EARLY = 26
FIRST = 4
NN = (((1,), (0,)), ((), ()))
NT = (((1,), (1,)), ((), ()))


def dot(left, right, dims):
    return lax.dot_general(left, right, dims, preferred_element_type=jnp.float32)


def thirds(value):
    high = value.astype(jnp.bfloat16).astype(jnp.float32)
    rest = value - high
    middle = rest.astype(jnp.bfloat16).astype(jnp.float32)
    low = rest - middle
    return jnp.concatenate([high, middle, low], axis=0).astype(jnp.bfloat16)


def joined(rows):
    return (rows[0:1] + rows[1:2]) + rows[2:3]


def far(size):
    return sorted(range(size), key=lambda step: -min(step, size - step))


def hops(step, size):
    return min(step, size - step)


def kernel(
    coupling_hbm,
    incidence_hbm,
    cost_hbm,
    capacity_hbm,
    demand_hbm,
    weights_hbm,
    slots_hbm,
    flows_out,
    duals_out,
    multipliers_out,
    consensus_out,
    squares_out,
    weight_out,
    flows_ref,
    duals_ref,
    multipliers_ref,
    consensus_ref,
    squares_ref,
    weight_ref,
    incidence,
    weights,
    cost_ref,
    capacity_ref,
    demand_ref,
    slots_ref,
    masked,
    turned,
    pick,
    fleet_columns,
    fleet_rows,
    loads,
    shares,
    fleet,
    all_duals,
    fetch_sem,
    store_sem,
    load_send,
    load_recv,
    share_send,
    share_recv,
    fleet_send,
    fleet_recv,
    square_send,
    square_recv,
):
    scen = lax.axis_index("scen")
    z = lax.axis_index("arc")
    x = scen // (NY * NC)
    y = (scen // NC) % NY
    core = scen % NC
    mine = y * NG + x * NC + core

    def at(dx, dy, dc):
        other = (lax.rem(x + dx, NX) * NY + lax.rem(y + dy, NY)) * NC + lax.rem(core + dc, NC)
        return (other, z)

    along_z = [(scen, lax.rem(z + step, NZ)) for step in far(NZ)[:-1]]
    group_steps = [(dx, 0, dc) for dx in far(NX) for dc in (1, 0) if dx + dc > 0]
    plane_steps = [(0, dy, 0) for dy in far(NY)[:-1]]
    group = [at(*step) for step in group_steps]
    plane = [at(*step) for step in plane_steps]
    steps = [(dx, dy, dc) for dx in range(NX) for dy in range(NY) for dc in range(NC)]
    steps = [s for s in steps if s != (0, 0, 0)]
    steps.sort(key=lambda s: -hops(s[0], NX) - hops(s[1], NY))

    barrier = pltpu.get_barrier_semaphore()
    greeted = [(hops(step, NZ), other) for step, other in zip(far(NZ), along_z)]
    greeted += [(hops(step[0], NX), other) for step, other in zip(group_steps, group)]
    greeted += [(hops(step[1], NY), other) for step, other in zip(plane_steps, plane)]
    greeted.sort(key=lambda entry: -entry[0])

    def greet(some):
        for _, other in some:
            pl.semaphore_signal(barrier, inc=1, device_id=other, device_id_type=MESH)

    greet(greeted[:FIRST])
    rows, arcs = masked.shape
    blocks = rows // TILE
    fleets = slots_ref.shape[1]
    depth = rows // CHUNKS
    fetches = []

    def fetch(source, target):
        copy = pltpu.make_async_copy(source, target, fetch_sem.at[len(fetches)])
        copy.start()
        fetches.append(copy)
        return copy

    fetch_incidence = fetch(incidence_hbm, incidence)
    fetch_cost = fetch(cost_hbm, cost_ref)
    fetch_capacity = fetch(capacity_hbm, capacity_ref)
    parts = [pl.ds(chunk * depth, depth) for chunk in range(CHUNKS)]
    fetch_masked = [fetch(coupling_hbm.at[part], masked.at[part]) for part in parts]
    greet(greeted[FIRST:])
    fetch_slots = fetch(slots_hbm, slots_ref)
    fetch_demand = fetch(demand_hbm, demand_ref)
    fetch_weights = fetch(weights_hbm, weights)

    def store(index, source, target):
        copy = pltpu.make_async_copy(source, target, store_sem.at[index])
        copy.start()
        return copy

    def send(source, target, partner, send_sem, recv_sem):
        pltpu.make_async_remote_copy(
            src_ref=source,
            dst_ref=target,
            send_sem=send_sem,
            recv_sem=recv_sem,
            device_id=partner,
            device_id_type=MESH,
        ).start()

    def awaited(rest, send_sem, recv_sem):
        return pltpu.make_async_remote_copy(
            src_ref=rest,
            dst_ref=rest,
            send_sem=send_sem,
            recv_sem=recv_sem,
            device_id=along_z[0],
            device_id_type=MESH,
        )

    def exchange(buffer, send_sem, recv_sem):
        for partner in along_z:
            send(buffer.at[z], buffer.at[z], partner, send_sem, recv_sem)
        return awaited(buffer.at[pl.ds(0, NZ - 1)], send_sem, recv_sem)

    fetch_cost.wait()
    fetch_capacity.wait()
    cost = cost_ref[...]
    capacity = capacity_ref[...]
    flows = jnp.clip(-primal_step * cost, 0.0, capacity)
    flows_bar = (2.0 * flows).astype(jnp.bfloat16)
    fetch_incidence.wait()
    for chunk, part in enumerate(parts):
        fetch_masked[chunk].wait()
        for row in range(chunk * depth // TILE, (chunk + 1) * depth // TILE):
            for column in range(arcs // TILE):
                tile = (pl.ds(row * TILE, TILE), pl.ds(column * TILE, TILE))
                factor = incidence[column, row].astype(jnp.float32)
                masked[tile] = masked[tile] * jnp.full((TILE, TILE), factor, jnp.float32).astype(jnp.bfloat16)
        load = dot(flows_bar, masked[part], NT)
        for i in range(depth // TILE):
            loads[0, z, pl.ds(chunk * depth // TILE + i, 1), :] = load[:, i * TILE : (i + 1) * TILE]
    pl.semaphore_wait(barrier, len(greeted))
    waits = [exchange(loads.at[0], load_send.at[0], load_recv.at[0])]

    fetch_weights.wait()
    own_row = pl.ds(mine, 1)
    shares[own_row, :] = jnp.full((1, fleets), weights[0].astype(jnp.float32))
    for partner in group:
        send(shares.at[own_row], shares.at[own_row], partner, share_send.at[0], share_recv.at[0])
    share_group = awaited(shares.at[pl.ds(0, NG - 1)], share_send.at[0], share_recv.at[0])
    for part in parts:
        turned[:, part] = masked[part].T
    fetch_slots.wait()
    places = lax.broadcasted_iota(jnp.int32, (arcs, fleets), 0)
    pick[...] = jnp.where(places == slots_ref[...], 1.0, 0.0).astype(jnp.bfloat16)
    is_fleet = dot(jnp.ones((1, fleets), jnp.bfloat16), pick[...], NT) > 0.5
    fetch_demand.wait()
    demand = demand_ref[...]

    def gathered(value):
        return joined(dot(thirds(value), pick[...], NN))

    def on_arcs(value):
        return joined(dot(thirds(value), pick[...], NT))

    def send_fleet(round_index, some_steps):
        line = fleet.at[round_index, own_row]
        for step in some_steps:
            send(line, line, at(*step), fleet_send.at[round_index], fleet_recv.at[round_index])

    def settle(round_index):
        arrival = awaited(
            fleet.at[round_index, pl.ds(0, SCEN - 1)], fleet_send.at[round_index], fleet_recv.at[round_index]
        )
        arrival.wait_recv()
        pending.append(arrival)
        return jnp.sum(shares[...] * fleet[round_index], axis=0, keepdims=True) / weight_sum

    def deviation(round_index, consensus):
        gap = fleet[round_index] - consensus
        return jnp.sum(shares[...] * gap * gap, axis=0, keepdims=True)

    def next_duals(duals, turn):
        waits[turn].wait_recv()
        row_load = loads[turn, 0]
        for i in range(1, NZ):
            row_load = row_load + loads[turn, i]
        return jnp.maximum(duals + dual_step * (row_load - demand), 0.0)

    fleet_columns[...] = dot(masked[...], pick[...], NN).astype(jnp.bfloat16)
    fleet_rows[...] = fleet_columns[...].T
    fleet_cost = gathered(cost)
    fleet_capacity = gathered(capacity)

    last_turn = ROUNDS * ITERS - 1
    duals = next_duals(jnp.zeros(demand.shape, jnp.float32), 0)
    multipliers = jnp.zeros((1, fleets), jnp.float32)
    consensus = jnp.zeros((1, fleets), jnp.float32)
    arc_multipliers = jnp.zeros((1, arcs), jnp.float32)
    arc_consensus = jnp.zeros((1, arcs), jnp.float32)
    deviations = []
    pending = []
    for turn in range(1, ROUNDS * ITERS):
        round_index = turn // ITERS
        row = jnp.concatenate([duals[i : i + 1] for i in range(blocks)], axis=1).astype(jnp.bfloat16)
        round_starts = turn % ITERS == 0
        round_ends = turn % ITERS == ITERS - 1
        later = []
        if round_starts or round_ends:
            fleet_gradient = fleet_cost + dot(row, fleet_columns[...], NN)
        if round_ends:
            fleet_gradient = fleet_gradient + (multipliers + penalty * (fleet_flow - consensus))
            fleet_flow = jnp.clip(fleet_flow - primal_step * fleet_gradient, 0.0, fleet_capacity)
            fleet[round_index, own_row, :] = fleet_flow
            early = len(steps) if turn == last_turn else EARLY
            send_fleet(round_index, steps[:early])
            later = steps[early:]
        gradient = cost + dot(row, masked[...], NN)
        if round_starts:
            flows_next = jnp.clip(flows - primal_step * gradient, 0.0, capacity)
            flows_bar = jnp.where(is_fleet, 0.0, 2.0 * flows_next - flows).astype(jnp.bfloat16)
            load = dot(flows_bar, turned[...], NN)
            consensus = settle(round_index - 1)
            multipliers = multipliers + penalty * (fleet_flow - consensus)
            fleet_gradient = fleet_gradient + (multipliers + penalty * (fleet_flow - consensus))
            fleet_next = jnp.clip(fleet_flow - primal_step * fleet_gradient, 0.0, fleet_capacity)
            fleet_bar = (2.0 * fleet_next - fleet_flow).astype(jnp.bfloat16)
            load = load + dot(fleet_bar, fleet_rows[...], NN)
        else:
            push = arc_multipliers + penalty * (flows - arc_consensus)
            gradient = gradient + jnp.where(is_fleet, push, 0.0)
            flows_next = jnp.clip(flows - primal_step * gradient, 0.0, capacity)
            flows_bar = (2.0 * flows_next - flows).astype(jnp.bfloat16)
            load = dot(flows_bar, turned[...], NN)
        for i in range(blocks):
            loads[turn, z, i : i + 1, :] = load[:, i * TILE : (i + 1) * TILE]
        waits.append(exchange(loads.at[turn], load_send.at[turn], load_recv.at[turn]))
        send_fleet(round_index, later)
        if round_starts:
            flows_next = jnp.where(is_fleet, on_arcs(fleet_next), flows_next)
            arc_consensus = on_arcs(consensus)
            arc_multipliers = on_arcs(multipliers)
            deviations.append(deviation(round_index - 1, consensus))
        flows = flows_next
        if turn % ITERS == ITERS - 2:
            fleet_flow = gathered(flows)
        if turn == 1:
            share_group.wait_recv()
            own_rows = pl.ds(pl.multiple_of(y * NG, NG), NG)
            for partner in plane:
                send(shares.at[own_rows], shares.at[own_rows], partner, share_send.at[1], share_recv.at[1])
            share_plane = awaited(shares.at[pl.ds(0, SCEN - NG)], share_send.at[1], share_recv.at[1])
        if turn == 2:
            share_plane.wait_recv()
            pending += [share_group, share_plane]
            weight_sum = jnp.sum(shares[...], axis=0, keepdims=True)
            weight_ref[...] = weight_sum
            stores = [store(5, weight_ref, weight_out)]
        if turn < last_turn:
            duals = next_duals(duals, turn)

    consensus = settle(ROUNDS - 1)
    deviations.append(deviation(ROUNDS - 1, consensus))
    squares_ref[...] = jnp.concatenate(deviations, axis=0)
    for partner in along_z:
        send(squares_ref, squares_out.at[z], partner, square_send, square_recv)
    wait = awaited(squares_out.at[pl.ds(0, NZ - 1)], square_send, square_recv)
    multipliers_ref[...] = multipliers + penalty * (fleet_flow - consensus)
    consensus_ref[...] = consensus
    flows_ref[...] = flows
    all_duals[...] = next_duals(duals, last_turn)
    duals_ref[...] = all_duals[pl.ds(z, 1), :]
    stores += [
        store(4, squares_ref, squares_out.at[z]),
        store(0, flows_ref, flows_out),
        store(1, duals_ref, duals_out),
        store(2, multipliers_ref, multipliers_out),
        store(3, consensus_ref, consensus_out),
    ]
    for done in waits + pending:
        done.wait_send()
    for done in stores:
        done.wait()
    wait.wait()


def place(
    flows,
    duals,
    multipliers,
    consensus,
    squares,
    weight,
    flows_out,
    duals_out,
    multipliers_out,
    consensus_out,
    spread_out,
    squares_ref,
    weight_ref,
    spread_ref,
    sem,
):
    pairs = [
        (squares, squares_ref),
        (weight, weight_ref),
        (flows, flows_out),
        (duals, duals_out),
        (multipliers, multipliers_out),
        (consensus, consensus_out),
    ]
    copies = [pltpu.make_async_copy(*pair, sem.at[i]) for i, pair in enumerate(pairs)]
    for copy in copies:
        copy.start()
    copies[0].wait()
    copies[1].wait()
    total = squares_ref[0]
    for i in range(1, NZ):
        total = total + squares_ref[i]
    total = jnp.sum(total, axis=1, keepdims=True)
    fleets = weight_ref.shape[1]
    spread = jnp.sqrt(total / (weight_ref[:, 0:1] * (fleets * NZ)) + 1e-06)
    spread_ref[...] = jnp.concatenate([spread[i : i + 1] for i in range(ROUNDS)], axis=1)
    last = pltpu.make_async_copy(spread_ref, spread_out, sem.at[len(pairs)])
    last.start()
    for copy in copies[2:]:
        copy.wait()
    last.wait()


def body(coupling, incidence, arc_cost, capacity, demand, weights, fleet_slots):
    rows, arcs = coupling.shape
    fleets = fleet_slots.shape[0]
    turns = ROUNDS * ITERS
    f32 = jnp.float32
    hbm = pl.BlockSpec(memory_space=pltpu.HBM)
    dma = pltpu.SemaphoreType.DMA
    outs = [
        jax.ShapeDtypeStruct((1, arcs), f32),
        jax.ShapeDtypeStruct((1, rows // NZ), f32),
        jax.ShapeDtypeStruct((1, fleets), f32),
        jax.ShapeDtypeStruct((1, fleets), f32),
    ]
    squares = jax.ShapeDtypeStruct((NZ, ROUNDS, fleets), f32)
    weight = jax.ShapeDtypeStruct((1, fleets), f32)
    spread = jax.ShapeDtypeStruct((1, ROUNDS), f32)
    results = pl.pallas_call(
        kernel,
        out_shape=outs + [squares, weight],
        in_specs=[hbm] * 7,
        out_specs=[hbm] * 6,
        scratch_shapes=[
            pltpu.VMEM((1, arcs), f32),
            pltpu.VMEM((1, rows // NZ), f32),
            pltpu.VMEM((1, fleets), f32),
            pltpu.VMEM((1, fleets), f32),
            pltpu.VMEM((ROUNDS, fleets), f32),
            pltpu.VMEM((1, fleets), f32),
            pltpu.SMEM((arcs // TILE, rows // TILE), jnp.int32),
            pltpu.SMEM((1,), jnp.int32),
            pltpu.VMEM((1, arcs), f32),
            pltpu.VMEM((1, arcs), f32),
            pltpu.VMEM((rows // TILE, TILE), f32),
            pltpu.VMEM((1, fleets), jnp.int32),
            pltpu.VMEM((rows, arcs), jnp.bfloat16),
            pltpu.VMEM((arcs, rows), jnp.bfloat16),
            pltpu.VMEM((arcs, fleets), jnp.bfloat16),
            pltpu.VMEM((rows, fleets), jnp.bfloat16),
            pltpu.VMEM((fleets, rows), jnp.bfloat16),
            pltpu.VMEM((turns, NZ, rows // TILE, TILE), f32),
            pltpu.VMEM((SCEN, fleets), f32),
            pltpu.VMEM((ROUNDS, SCEN, fleets), f32),
            pltpu.VMEM((rows // TILE, TILE), f32),
            dma((6 + CHUNKS,)),
            dma((6,)),
            dma((turns,)),
            dma((turns,)),
            dma((2,)),
            dma((2,)),
            dma((ROUNDS,)),
            dma((ROUNDS,)),
            dma,
            dma,
        ],
        compiler_params=pltpu.CompilerParams(
            collective_id=0, has_side_effects=True, vmem_limit_bytes=60 * 1024 * 1024
        ),
        cost_estimate=pl.CostEstimate(
            flops=4 * turns * rows * arcs, bytes_accessed=2 * rows * arcs, transcendentals=0
        ),
    )(
        coupling,
        incidence.T,
        arc_cost.reshape(1, arcs),
        capacity.reshape(1, arcs),
        demand.reshape(rows // TILE, TILE),
        weights,
        fleet_slots.reshape(1, fleets),
    )
    flows, duals, multipliers, consensus, spread = pl.pallas_call(
        place,
        out_shape=outs + [spread],
        in_specs=[hbm] * 6,
        out_specs=[hbm] * 5,
        scratch_shapes=[
            pltpu.VMEM(squares.shape, f32),
            pltpu.VMEM(weight.shape, f32),
            pltpu.VMEM(spread.shape, f32),
            dma((7,)),
        ],
    )(*results)
    return flows, duals, multipliers, consensus.reshape(fleets), spread.reshape(ROUNDS)


def solution(mesh):
    in_specs = (
        P(None, "arc"),
        P(None, "arc"),
        P("arc"),
        P("arc"),
        P("scen", None),
        P("scen"),
        P("arc"),
    )
    out_specs = (P("scen", "arc"), P("scen", "arc"), P("scen", "arc"), P("arc"), P())
    return jax.shard_map(body, mesh=mesh, in_specs=in_specs, out_specs=out_specs, check_vma=False)
```
